32 devices in a mesh: gz: 8 (over z, y), row: 4 (over x, core).
Axes of the slice: x: 2, y: 2, z: 4, core: 2. Of those that a mesh axis runs over, the one named last changes fastest.
Arguments:
- density: float32 [64, 32, 256], P('gz', 'row'), may hold values from 0.3 to 3
- pressure: float32 [64, 32, 256], P('gz', 'row'), may hold values from 0.3 to 3
- velocity: float32 [3, 64, 32, 256], P(None, 'gz', 'row'), may hold values from -3 to 3
- boundary: int32 [6], replicated, may hold values from 0 to 1
Outputs:
- density_out: float32 [64, 32, 256], P('gz', 'row')
- pressure_out: float32 [64, 32, 256], P('gz', 'row')
- velocity_out: float32 [3, 64, 32, 256], P(None, 'gz', 'row')
The draws below stay inside these ranges and needn't reach their ends.
Inputs may be any that keep to these rules, and one draw needn't show every extreme that they name: `boundary`: 1 marks a reflecting face, 0 an outflow face; entries 2k and 2k+1 are the lower and upper faces of x, y, z in turn.
All inputs are finite; a program needn't handle non-finite values.
Results may differ from the reference program's by a relative error of at most 0.0003.
Values sent between devices are 32-bit elements; how exact they have to be, the bound alone decides.
A program may use at most 64 MiB of HBM per device.

```python
import math
import jax
import jax.numpy as jnp
import numpy as np
from jax import lax

NX = 256
RIEMANN_ITERS = 4
NY = 32
NZ = 64


def place_ends(entries, key, low, largest):
    longest = entries.shape.index(max(entries.shape))
    spots = []
    for shift in (0, 1):
        where = [jax.random.randint(jax.random.fold_in(key, axis), (), 0, length) for axis, length in enumerate(entries.shape)]
        where[longest] = (where[longest] + shift) % entries.shape[longest]
        spots.append(tuple(where))
    return entries.at[spots[0]].set(low).at[spots[1]].set(largest)


def level_of(stream_key, extent, pieces, low, high):
    factor_of = 1.0
    for dim, blocks in pieces:
        draws = jax.random.uniform(jax.random.fold_in(jax.random.fold_in(stream_key, 6), dim), (blocks,), jnp.float32, low / len(pieces), high / len(pieces))
        factor_of = factor_of * jnp.repeat(jnp.exp(draws), extent[dim] // blocks).reshape((-1,) + (1,) * (len(extent) - 1 - dim))
    return factor_of


def centred(rng, shape, deviation, most, pieces=(), held_as=jnp.bfloat16):
    result = deviation * jax.random.normal(rng, shape, jnp.float32)
    if pieces:
        result = result * level_of(rng, shape, pieces, -0.22, 0.18)
    return jnp.clip(result, -most, most).astype(held_as)


def setup_inputs(seed: int = 0) -> dict:
    arg_keys = jax.random.split(jax.random.key(seed), 5)
    density = jnp.clip(jnp.exp(math.log(3.0) - 2.3025851 * jax.random.uniform(arg_keys[0], (NZ, NY, NX), jnp.float32) ** level_of(arg_keys[0], (NZ, NY, NX), ((0, 8), (1, 4)), -0.2, 0.2)), 0.3, 3.0)
    pressure = jnp.clip(jnp.exp(math.log(3.0) - 2.3025851 * jax.random.uniform(arg_keys[1], (NZ, NY, NX), jnp.float32) ** level_of(arg_keys[1], (NZ, NY, NX), ((0, 8), (1, 4)), -0.2, 0.2)), 0.3, 3.0)
    velocity = centred(arg_keys[2], (3, NZ, NY, NX), 0.5, 3.0, ((1, 8), (2, 4)), jnp.float32)
    boundary = place_ends(jax.random.randint(arg_keys[3], (6,), 0, 2), jax.random.fold_in(arg_keys[3], 1), 0, 1).astype(jnp.int32)
    return {"density": density, "pressure": pressure, "velocity": velocity, "boundary": boundary}


gamma_gas = 1.4
courant_ratio = 0.05
dens_floor = 0.02
press_floor = 0.02
star_frac = 0.1

def mirror_sign(normal, ndim):
    table = np.ones(5, np.float32)
    table[normal] = -1.0
    return jnp.asarray(table.reshape((5,) + (1,) * (ndim - 1)))

def normal_mask(normal, ndim):
    table = np.zeros(3, np.float32)
    table[normal - 2] = 1.0
    return jnp.asarray(table.reshape((3,) + (1,) * (ndim - 1)))

def boundary_cells(interior, along, face_flag, at_lower, normal):
    reflect = jnp.flip(interior, axis=along) * mirror_sign(normal, interior.ndim)
    edge_index = 0 if at_lower else 2
    edge_cell = lax.slice_in_dim(interior, edge_index, edge_index + 1, axis=along)
    outflow = jnp.concatenate([edge_cell, edge_cell, edge_cell], axis=along)
    return jnp.where(face_flag == 1, reflect, outflow)

def add_ghosts(fields, along, low_flag, high_flag, normal):
    inner_len = fields.shape[along]
    lower_ghosts = boundary_cells(lax.slice_in_dim(fields, 0, 3, axis=along), along, low_flag, True, normal)
    upper_ghosts = boundary_cells(lax.slice_in_dim(fields, inner_len - 3, inner_len, axis=along), along, high_flag, False, normal)
    return jnp.concatenate([lower_ghosts, fields, upper_ghosts], axis=along)

def conserved(prims):
    dens = prims[0:1]
    speeds = prims[2:5]
    energy = prims[1:2] / (gamma_gas - 1.0) + 0.5 * dens * lax.optimization_barrier(jnp.sum(speeds * speeds, axis=0, keepdims=True))
    return jnp.concatenate([dens, energy, dens * speeds], axis=0)

def primitive(conserv):
    dens = jnp.maximum(conserv[0:1], dens_floor)
    speeds = conserv[2:5] / dens
    press = (gamma_gas - 1.0) * (conserv[1:2] - 0.5 * dens * lax.optimization_barrier(jnp.sum(speeds * speeds, axis=0, keepdims=True)))
    return jnp.concatenate([dens, jnp.maximum(press, press_floor), speeds], axis=0)

def shock_side(star_press, side_press, sound_imp):
    ratio_g = (gamma_gas + 1.0) / (2.0 * gamma_gas)
    wave_speed = sound_imp * jnp.sqrt(1.0 + ratio_g * (star_press / side_press - 1.0))
    jump_speed = (star_press - side_press) / wave_speed
    jump_slope = sound_imp * sound_imp * (1.0 + ratio_g * (star_press - side_press) / (2.0 * side_press)) / wave_speed ** 3
    return (jump_speed, jump_slope)

def godunov(left_state, right_state, normal):
    dens_left, dens_right = (left_state[0], right_state[0])
    press_left, press_right = (left_state[1], right_state[1])
    normal_left, normal_right = (left_state[normal], right_state[normal])
    sound_left = jnp.sqrt(gamma_gas * press_left * dens_left)
    sound_right = jnp.sqrt(gamma_gas * press_right * dens_right)
    floor_press = star_frac * jnp.minimum(press_left, press_right)
    star_press = (sound_right * press_left + sound_left * press_right - sound_left * sound_right * (normal_right - normal_left)) / (sound_left + sound_right)
    star_press = jnp.maximum(star_press, floor_press)
    for attempt in range(RIEMANN_ITERS):
        jump_left, slope_left = shock_side(star_press, press_left, sound_left)
        jump_right, slope_right = shock_side(star_press, press_right, sound_right)
        star_press = star_press - (normal_right - normal_left + jump_left + jump_right) / (slope_left + slope_right)
        star_press = jnp.maximum(star_press, floor_press)
    jump_left, slope_left = shock_side(star_press, press_left, sound_left)
    jump_right, slope_right = shock_side(star_press, press_right, sound_right)
    star_speed = 0.5 * (normal_left - jump_left + (normal_right + jump_right))
    upwind = star_speed > 0.0
    dens_up = jnp.where(upwind, dens_left, dens_right)
    press_up = jnp.where(upwind, press_left, press_right)
    selector = normal_mask(normal, left_state.ndim)
    vel_up = jnp.where(upwind[None], left_state[2:5], right_state[2:5])
    vel_up = selector * star_speed[None] + (1.0 - selector) * vel_up
    energy_up = press_up / (gamma_gas - 1.0) + 0.5 * dens_up * lax.optimization_barrier(jnp.sum(vel_up * vel_up, axis=0))
    mass_flux = dens_up * star_speed
    energy_flux = (energy_up + star_press) * star_speed
    moment_flux = mass_flux[None] * vel_up + selector * star_press[None]
    return jnp.concatenate([mass_flux[None], energy_flux[None], moment_flux], axis=0)

def sweep_cells(padded, along, normal):
    inner_len = padded.shape[along] - 6

    def window(start, length):
        return lax.slice_in_dim(padded, start, start + length, axis=along)
    left_in = window(1, inner_len + 3)
    right_in = window(2, inner_len + 3)
    interfaces = (7.0 * (left_in + right_in) - (window(0, inner_len + 3) + window(3, inner_len + 3))) / 12.0
    interfaces = jnp.clip(interfaces, jnp.minimum(left_in, right_in), jnp.maximum(left_in, right_in))
    centres = window(2, inner_len + 2)
    to_left = lax.slice_in_dim(interfaces, 0, inner_len + 2, axis=along) - centres
    to_right = lax.slice_in_dim(interfaces, 1, inner_len + 3, axis=along) - centres
    west_edge = centres + jnp.clip(to_left, -2.0 * jnp.abs(to_right), 2.0 * jnp.abs(to_right))
    east_edge = centres + jnp.clip(to_right, -2.0 * jnp.abs(to_left), 2.0 * jnp.abs(to_left))
    left_state = lax.slice_in_dim(east_edge, 0, inner_len + 1, axis=along)
    right_state = lax.slice_in_dim(west_edge, 1, inner_len + 2, axis=along)
    fluxes = godunov(left_state, right_state, normal)
    conserv = conserved(window(3, inner_len))
    conserv = conserv - courant_ratio * (lax.slice_in_dim(fluxes, 1, inner_len + 1, axis=along) - lax.slice_in_dim(fluxes, 0, inner_len, axis=along))
    return primitive(conserv)

def reference(density, pressure, velocity, boundary):
    fields = jnp.concatenate([density[None], pressure[None], velocity], axis=0)
    planes = jnp.transpose(fields, (1, 0, 2, 3))

    def xy_sweeps(plane_cut):
        plane_cut = sweep_cells(add_ghosts(plane_cut, 2, boundary[0], boundary[1], 2), 2, 2)
        return sweep_cells(add_ghosts(plane_cut, 1, boundary[2], boundary[3], 3), 1, 3)
    planes = lax.map(xy_sweeps, planes)
    row_cuts = jnp.transpose(planes, (2, 1, 0, 3))

    def z_sweep(column_cut):
        return sweep_cells(add_ghosts(column_cut, 1, boundary[4], boundary[5], 4), 1, 4)
    row_cuts = lax.map(z_sweep, row_cuts)
    fields = jnp.transpose(row_cuts, (1, 2, 0, 3))
    return (fields[0], fields[1], fields[2:5])
```

```python
import functools

import jax
import jax.numpy as jnp
from jax import lax
from jax.experimental import pallas as pl
from jax.experimental.pallas import tpu as pltpu
from jax.sharding import PartitionSpec as P

RIEMANN_ITERS = 4
GAMMA = 1.4
COURANT = 0.05
DENS_FLOOR = 0.02
PRESS_FLOOR = 0.02
STAR_FRAC = 0.1
RATIO = (GAMMA + 1.0) / (2.0 * GAMMA)
LANES = 128
SUBS = 8
FIELDS = 5


def rough_inverse(x):
    return pl.reciprocal(x, approx=True)


def inverse(x):
    y = rough_inverse(x)
    return y * (2.0 - x * y)


def clip_between(x, a, b):
    return jnp.minimum(jnp.maximum(x, jnp.minimum(a, b)), jnp.maximum(a, b))


def edge_pair(centre, lower, upper):
    dl = lower - centre
    dr = upper - centre
    rl = 2.0 * jnp.abs(dl)
    rr = 2.0 * jnp.abs(dr)
    west = centre + jnp.minimum(jnp.maximum(dl, -rr), rr)
    east = centre + jnp.minimum(jnp.maximum(dr, -rl), rl)
    return west, east


def interface(far_left, left, right, far_right):
    value = (7.0 * (left + right) - (far_left + far_right)) * (1.0 / 12.0)
    return clip_between(value, left, right)


def riemann_flux(left, right, normal):
    rho_l, p_l, u_l = left[0], left[1], left[normal]
    rho_r, p_r, u_r = right[0], right[1], right[normal]
    inv_c_l = lax.rsqrt(GAMMA * p_l * rho_l)
    inv_c_r = lax.rsqrt(GAMMA * p_r * rho_r)
    slope_l = RATIO * inverse(p_l)
    slope_r = RATIO * inverse(p_r)
    du = u_r - u_l
    floor = STAR_FRAC * jnp.minimum(p_l, p_r)
    star = (p_l * inv_c_l + p_r * inv_c_r - du) * inverse(inv_c_l + inv_c_r)
    star = jnp.maximum(star, floor)

    def jump(star, p, inv_c, slope):
        r = lax.rsqrt((1.0 - RATIO) + slope * star)
        t = inv_c * r
        return (star - p) * t, r, t

    for _ in range(RIEMANN_ITERS):
        f_l, r_l, t_l = jump(star, p_l, inv_c_l, slope_l)
        f_r, r_r, t_r = jump(star, p_r, inv_c_r, slope_r)
        twice = t_l * (1.0 + r_l * r_l) + t_r * (1.0 + r_r * r_r)
        total = du + f_l + f_r
        star = star - (total + total) * rough_inverse(twice)
        star = jnp.maximum(star, floor)
    f_l, _, _ = jump(star, p_l, inv_c_l, slope_l)
    f_r, _, _ = jump(star, p_r, inv_c_r, slope_r)
    speed = 0.5 * ((u_l - f_l) + (u_r + f_r))
    up = speed > 0.0
    vel = [speed if a == normal else jnp.where(up, left[a], right[a]) for a in (2, 3, 4)]
    rho = jnp.where(up, rho_l, rho_r)
    press = jnp.where(up, p_l, p_r)
    energy = press * (1.0 / (GAMMA - 1.0)) + 0.5 * rho * (
        vel[0] * vel[0] + vel[1] * vel[1] + vel[2] * vel[2]
    )
    mass = rho * speed
    flux = [mass, (energy + star) * speed] + [mass * v for v in vel]
    flux[normal] = flux[normal] + star
    return flux


def advance(cells, low, high):
    rho, press = cells[0], cells[1]
    vel = cells[2:5]
    energy = press * (1.0 / (GAMMA - 1.0)) + 0.5 * rho * (
        vel[0] * vel[0] + vel[1] * vel[1] + vel[2] * vel[2]
    )
    old = [rho, energy] + [rho * v for v in vel]
    new = [o - COURANT * (h - l) for o, h, l in zip(old, high, low)]
    rho = jnp.maximum(new[0], DENS_FLOOR)
    inv = inverse(rho)
    vel = [m * inv for m in new[2:5]]
    press = (GAMMA - 1.0) * (
        new[1] - 0.5 * rho * (vel[0] * vel[0] + vel[1] * vel[1] + vel[2] * vel[2])
    )
    return [rho, jnp.maximum(press, PRESS_FLOOR)] + vel


def lane_roll(a, shift):
    if shift % LANES == 0:
        return a
    flat = a.reshape(-1, LANES)
    return pltpu.roll(flat, shift % LANES, 1).reshape(a.shape)


def from_below(a, fill):
    lane = lax.broadcasted_iota(jnp.int32, a.shape, 3)
    rolled = lane_roll(a, 1)
    other = jnp.concatenate([fill, rolled[:, :-1]], axis=1)
    return jnp.where(lane == 0, other, rolled)


def from_above(a, fill):
    lane = lax.broadcasted_iota(jnp.int32, a.shape, 3)
    rolled = lane_roll(a, LANES - 1)
    other = jnp.concatenate([rolled[:, 1:], fill], axis=1)
    return jnp.where(lane == LANES - 1, other, rolled)


def x_sweep(cells, sign_low, sign_high):
    rows, halves = cells[0].shape[:2]
    lane = lax.broadcasted_iota(jnp.int32, (1, SUBS, LANES), 2)
    left, right = [], []
    for f, a in enumerate(cells):
        s_low = sign_low if f == 2 else 1.0
        s_high = sign_high if f == 2 else 1.0
        below = from_below(a, s_low * a[:, :1])
        above = from_above(a, s_high * a[:, -1:])
        above2 = from_above(above, s_high * below[:, -1:])
        upper = interface(below, a, above, above2)
        lower = from_below(upper, 0.5 * (a[:, :1] + s_low * a[:, :1]))
        west, east = edge_pair(a, lower, upper)
        west_next = from_above(west, s_high * east[:, -1:])
        first = west[0, :1]
        for r in range(1, rows):
            first = jnp.where(lane == r, lane_roll(west[r, :1], r), first)
        count = rows * halves
        left.append(
            jnp.concatenate([east.reshape(count, SUBS, LANES), s_low * first], axis=0)
        )
        right.append(jnp.concatenate([west_next.reshape(count, SUBS, LANES), first], axis=0))
    flux = riemann_flux(left, right, 2)
    low, high = [], []
    for f in range(FIELDS):
        upper = flux[f][:-1].reshape(rows, halves, SUBS, LANES)
        faces = flux[f][-1:]
        fill = jnp.stack([lane_roll(faces, -r) for r in range(rows)], axis=0)
        low.append(from_below(upper, fill))
        high.append(upper)
    return advance(cells, low, high)


def line_flux(cells, normal):
    left, right = [], []
    for a in cells:
        inter = interface(a[:, :-3], a[:, 1:-2], a[:, 2:-1], a[:, 3:])
        west, east = edge_pair(a[:, 2:-2], inter[:, :-1], inter[:, 1:])
        left.append(east[:, :-1])
        right.append(west[:, 1:])
    return riemann_flux(left, right, normal)


def kernel(
    sizes,
    flags,
    dens_in,
    press_in,
    vel_in,
    dens_out,
    press_out,
    vel_out,
    held,
    ypad,
    zpad,
    done,
    in_sem,
    y_send,
    y_recv,
    z_send,
    z_recv,
    out_sem,
):
    planes, rows, halves = sizes
    cells = planes * rows
    step = FIELDS * SUBS
    row, row_count = lax.axis_index("row"), lax.axis_size("row")
    gz, gz_count = lax.axis_index("gz"), lax.axis_size("gz")

    def view(dens, press, vel, f, h):
        ref = (dens, press, vel, vel, vel)[f]
        start = max(f - 2, 0) * cells
        return ref.at[pl.ds(start, cells), pl.ds(h * LANES, LANES)]

    loads = [
        pltpu.make_async_copy(
            view(dens_in, press_in, vel_in, f, h), held.at[f, h], in_sem.at[f, h]
        )
        for f in range(FIELDS)
        for h in range(halves)
    ]
    for copy in loads:
        copy.start()

    barrier = pltpu.get_barrier_semaphore()
    sides = (
        (row > 0, {"row": row - 1}),
        (row < row_count - 1, {"row": row + 1}),
        (gz > 0, {"gz": gz - 1}),
        (gz < gz_count - 1, {"gz": gz + 1}),
    )
    for there, device in sides:

        @pl.when(there)
        def _(device=device):
            pl.semaphore_signal(
                barrier, inc=1, device_id=device, device_id_type=pl.DeviceIdType.MESH
            )

    for copy in loads:
        copy.wait()

    signs = [jnp.where(flags[k] == 1, -1.0, 1.0).astype(jnp.float32) for k in range(6)]

    def swept_rows(which):
        here = [
            jnp.stack(
                [
                    jnp.stack(
                        [held[f, h, pl.ds(r, SUBS, stride=rows), :] for h in range(halves)],
                        axis=0,
                    )
                    for r in which
                ],
                axis=0,
            )
            for f in range(FIELDS)
        ]
        new = x_sweep(here, signs[0], signs[1])
        for f in range(FIELDS):
            for i, r in enumerate(which):
                for h in range(halves):
                    ypad[h, 3 + r, f] = new[f][i, h]

    def y_copy(up, h):
        source, target = (rows, 0) if up else (3, rows + 3)
        return pltpu.make_async_remote_copy(
            src_ref=ypad.at[h, pl.ds(source, 3)],
            dst_ref=ypad.at[h, pl.ds(target, 3)],
            send_sem=y_send.at[up, h],
            recv_sem=y_recv.at[up, h],
            device_id={"row": row + (1 if up else -1)},
            device_id_type=pl.DeviceIdType.MESH,
        )

    def z_copy(up, h):
        source, target = (planes, 0) if up else (3, planes + 3)
        return pltpu.make_async_remote_copy(
            src_ref=zpad.at[h, pl.ds(source * step, 3 * step)],
            dst_ref=zpad.at[h, pl.ds(target * step, 3 * step)],
            send_sem=z_send.at[up, h],
            recv_sem=z_recv.at[up, h],
            device_id={"gz": gz + (1 if up else -1)},
            device_id_type=pl.DeviceIdType.MESH,
        )

    row_up, row_down = row < row_count - 1, row > 0
    gz_up, gz_down = gz < gz_count - 1, gz > 0

    swept_rows(list(range(rows - 3, rows)))
    pl.semaphore_wait(barrier, sum(there.astype(jnp.int32) for there, _ in sides))

    @pl.when(row_up)
    def _():
        for h in range(halves):
            y_copy(1, h).start()

    swept_rows([0, 1, 2])

    @pl.when(row_down)
    def _():
        for h in range(halves):
            y_copy(0, h).start()

    swept_rows(list(range(3, rows - 3)))

    def ghosts(get, put, count, normal, sign, upper):
        for f in range(FIELDS):
            for k in (1, 2, 3):
                inside = count + 3 - k if upper else 2 + k
                edge = count + 2 if upper else 3
                outside = count + 2 + k if upper else 3 - k
                mirror = get(inside, f)
                if f == normal:
                    mirror = -mirror
                put(outside, f, jnp.where(sign < 0.0, mirror, get(edge, f)))

    def y_get(h, j, f):
        return ypad[h, j, f]

    def y_put(h, j, f, value):
        ypad[h, j, f] = value

    def z_get(h, j, f):
        return zpad[h, pl.ds(j * step + f * SUBS, SUBS), :]

    def z_put(h, j, f, value):
        zpad[h, pl.ds(j * step + f * SUBS, SUBS), :] = value

    def swept_line(get, count, normal, arrived, finish):
        def block(h, start, stop):
            return [
                jnp.stack([get(h, j, f) for j in range(start, stop)], axis=0)
                for f in range(FIELDS)
            ]

        blocks = [block(h, 3, count + 3) for h in range(halves)]
        inner = line_flux([jnp.stack(a, axis=0) for a in zip(*blocks)], normal)
        for h in range(halves):
            arrived(h)
            ends = [block(h, 0, 8), block(h, count - 2, count + 6)]
            outer = line_flux([jnp.stack(a, axis=0) for a in zip(*ends)], normal)
            faces = [
                jnp.concatenate([o[0], i[h], o[1]], axis=0) for o, i in zip(outer, inner)
            ]
            new = advance(
                block(h, 3, count + 3), [a[:-1] for a in faces], [a[1:] for a in faces]
            )
            finish(h, new)

    def arrival(copy, get, put, down, up, count, normal, sign_low, sign_high, h):
        @pl.when(down)
        def _():
            copy(1, h).wait_recv()

        @pl.when(jnp.logical_not(down))
        def _():
            ghosts(
                functools.partial(get, h),
                functools.partial(put, h),
                count,
                normal,
                sign_low,
                False,
            )

        @pl.when(up)
        def _():
            copy(0, h).wait_recv()

        @pl.when(jnp.logical_not(up))
        def _():
            ghosts(
                functools.partial(get, h),
                functools.partial(put, h),
                count,
                normal,
                sign_high,
                True,
            )

    def y_finish(h, new):
        for f in range(FIELDS):
            for r in range(rows):
                zpad[h, pl.ds(3 * step + f * SUBS + r, planes, stride=step), :] = new[f][r]

        @pl.when(gz_up)
        def _():
            z_copy(1, h).start()

        @pl.when(gz_down)
        def _():
            z_copy(0, h).start()

    swept_line(
        y_get,
        rows,
        3,
        functools.partial(
            arrival, y_copy, y_get, y_put, row_down, row_up, rows, 3, signs[2], signs[3]
        ),
        y_finish,
    )

    def out_copy(f, h):
        return pltpu.make_async_copy(
            done.at[f, h], view(dens_out, press_out, vel_out, f, h), out_sem.at[f, h]
        )

    def z_finish(h, new):
        for f in range(FIELDS):
            done[f, h] = new[f].reshape(cells, LANES)
            out_copy(f, h).start()

    swept_line(
        z_get,
        planes,
        4,
        functools.partial(
            arrival, z_copy, z_get, z_put, gz_down, gz_up, planes, 4, signs[4], signs[5]
        ),
        z_finish,
    )

    for there, copy, up in (
        (row_up, y_copy, 1),
        (row_down, y_copy, 0),
        (gz_up, z_copy, 1),
        (gz_down, z_copy, 0),
    ):

        @pl.when(there)
        def _(copy=copy, up=up):
            for h in range(halves):
                copy(up, h).wait_send()

    for f in range(FIELDS):
        for h in range(halves):
            out_copy(f, h).wait()


def on_device(density, pressure, velocity, boundary):
    planes, rows, width = density.shape
    cells, halves = planes * rows, width // LANES
    scalar = jax.ShapeDtypeStruct((cells, width), jnp.float32)
    vector = jax.ShapeDtypeStruct((3 * cells, width), jnp.float32)
    anywhere = pl.BlockSpec(memory_space=pl.ANY)
    dens, press, vel = pl.pallas_call(
        functools.partial(kernel, (planes, rows, halves)),
        out_shape=(scalar, scalar, vector),
        in_specs=[pl.BlockSpec(memory_space=pltpu.SMEM)] + [anywhere] * 3,
        out_specs=(anywhere, anywhere, anywhere),
        scratch_shapes=[
            pltpu.VMEM((FIELDS, halves, cells, LANES), jnp.float32),
            pltpu.VMEM((halves, rows + 6, FIELDS, planes, LANES), jnp.float32),
            pltpu.VMEM((halves, (planes + 6) * FIELDS * rows, LANES), jnp.float32),
            pltpu.VMEM((FIELDS, halves, cells, LANES), jnp.float32),
            pltpu.SemaphoreType.DMA((FIELDS, halves)),
            pltpu.SemaphoreType.DMA((2, halves)),
            pltpu.SemaphoreType.DMA((2, halves)),
            pltpu.SemaphoreType.DMA((2, halves)),
            pltpu.SemaphoreType.DMA((2, halves)),
            pltpu.SemaphoreType.DMA((FIELDS, halves)),
        ],
        compiler_params=pltpu.CompilerParams(
            collective_id=0, has_side_effects=True, vmem_limit_bytes=32 * 1024 * 1024
        ),
    )(
        boundary,
        density.reshape(cells, width),
        pressure.reshape(cells, width),
        velocity.reshape(3 * cells, width),
    )
    return (
        dens.reshape(planes, rows, width),
        press.reshape(planes, rows, width),
        vel.reshape(3, planes, rows, width),
    )


def solution(mesh):
    in_specs = (P("gz", "row", None), P("gz", "row", None), P(None, "gz", "row", None), P())
    out_specs = (P("gz", "row", None), P("gz", "row", None), P(None, "gz", "row", None))
    return jax.shard_map(
        on_device, mesh=mesh, in_specs=in_specs, out_specs=out_specs, check_vma=False
    )
```

```python
import functools

import jax
import jax.numpy as jnp
from jax import lax
from jax.experimental import pallas as pl
from jax.experimental.pallas import tpu as pltpu
from jax.sharding import PartitionSpec as P

RIEMANN_ITERS = 4
GAMMA = 1.4
COURANT = 0.05
DENS_FLOOR = 0.02
PRESS_FLOOR = 0.02
STAR_FRAC = 0.1
RATIO = (GAMMA + 1.0) / (2.0 * GAMMA)
LANES = 128
SUBS = 8
FIELDS = 5


def rough_inverse(x):
    return pl.reciprocal(x, approx=True)


def inverse(x):
    y = rough_inverse(x)
    return y * (2.0 - x * y)


def clip_between(x, a, b):
    return jnp.minimum(jnp.maximum(x, jnp.minimum(a, b)), jnp.maximum(a, b))


def edge_pair(centre, lower, upper):
    dl = lower - centre
    dr = upper - centre
    rl = 2.0 * jnp.abs(dl)
    rr = 2.0 * jnp.abs(dr)
    west = centre + jnp.minimum(jnp.maximum(dl, -rr), rr)
    east = centre + jnp.minimum(jnp.maximum(dr, -rl), rl)
    return west, east


def interface(far_left, left, right, far_right):
    value = (7.0 * (left + right) - (far_left + far_right)) * (1.0 / 12.0)
    return clip_between(value, left, right)


def riemann_flux(left, right, normal):
    rho_l, p_l, u_l = left[0], left[1], left[normal]
    rho_r, p_r, u_r = right[0], right[1], right[normal]
    inv_c_l = lax.rsqrt(GAMMA * p_l * rho_l)
    inv_c_r = lax.rsqrt(GAMMA * p_r * rho_r)
    slope_l = RATIO * inverse(p_l)
    slope_r = RATIO * inverse(p_r)
    du = u_r - u_l
    floor = STAR_FRAC * jnp.minimum(p_l, p_r)
    star = (p_l * inv_c_l + p_r * inv_c_r - du) * inverse(inv_c_l + inv_c_r)
    star = jnp.maximum(star, floor)

    def jump(star, p, inv_c, slope):
        r = lax.rsqrt((1.0 - RATIO) + slope * star)
        t = inv_c * r
        return (star - p) * t, r, t

    for _ in range(RIEMANN_ITERS):
        f_l, r_l, t_l = jump(star, p_l, inv_c_l, slope_l)
        f_r, r_r, t_r = jump(star, p_r, inv_c_r, slope_r)
        twice = t_l * (1.0 + r_l * r_l) + t_r * (1.0 + r_r * r_r)
        total = du + f_l + f_r
        star = star - (total + total) * rough_inverse(twice)
        star = jnp.maximum(star, floor)
    f_l, _, _ = jump(star, p_l, inv_c_l, slope_l)
    f_r, _, _ = jump(star, p_r, inv_c_r, slope_r)
    speed = 0.5 * ((u_l - f_l) + (u_r + f_r))
    up = speed > 0.0
    vel = [speed if a == normal else jnp.where(up, left[a], right[a]) for a in (2, 3, 4)]
    rho = jnp.where(up, rho_l, rho_r)
    press = jnp.where(up, p_l, p_r)
    energy = press * (1.0 / (GAMMA - 1.0)) + 0.5 * rho * (
        vel[0] * vel[0] + vel[1] * vel[1] + vel[2] * vel[2]
    )
    mass = rho * speed
    flux = [mass, (energy + star) * speed] + [mass * v for v in vel]
    flux[normal] = flux[normal] + star
    return flux


def advance(cells, low, high):
    rho, press = cells[0], cells[1]
    vel = cells[2:5]
    energy = press * (1.0 / (GAMMA - 1.0)) + 0.5 * rho * (
        vel[0] * vel[0] + vel[1] * vel[1] + vel[2] * vel[2]
    )
    old = [rho, energy] + [rho * v for v in vel]
    new = [o - COURANT * (h - l) for o, h, l in zip(old, high, low)]
    rho = jnp.maximum(new[0], DENS_FLOOR)
    inv = inverse(rho)
    vel = [m * inv for m in new[2:5]]
    press = (GAMMA - 1.0) * (
        new[1] - 0.5 * rho * (vel[0] * vel[0] + vel[1] * vel[1] + vel[2] * vel[2])
    )
    return [rho, jnp.maximum(press, PRESS_FLOOR)] + vel


def lane_roll(a, shift):
    if shift % LANES == 0:
        return a
    flat = a.reshape(-1, LANES)
    return pltpu.roll(flat, shift % LANES, 1).reshape(a.shape)


def from_below(a, fill):
    lane = lax.broadcasted_iota(jnp.int32, a.shape, 3)
    rolled = lane_roll(a, 1)
    other = jnp.concatenate([fill, rolled[:, :-1]], axis=1)
    return jnp.where(lane == 0, other, rolled)


def from_above(a, fill):
    lane = lax.broadcasted_iota(jnp.int32, a.shape, 3)
    rolled = lane_roll(a, LANES - 1)
    other = jnp.concatenate([rolled[:, 1:], fill], axis=1)
    return jnp.where(lane == LANES - 1, other, rolled)


def x_sweep(cells, sign_low, sign_high):
    rows, halves = cells[0].shape[:2]
    lane = lax.broadcasted_iota(jnp.int32, (1, SUBS, LANES), 2)
    left, right = [], []
    for f, a in enumerate(cells):
        s_low = sign_low if f == 2 else 1.0
        s_high = sign_high if f == 2 else 1.0
        below = from_below(a, s_low * a[:, :1])
        above = from_above(a, s_high * a[:, -1:])
        above2 = from_above(above, s_high * below[:, -1:])
        upper = interface(below, a, above, above2)
        lower = from_below(upper, 0.5 * (a[:, :1] + s_low * a[:, :1]))
        west, east = edge_pair(a, lower, upper)
        west_next = from_above(west, s_high * east[:, -1:])
        first = west[0, :1]
        for r in range(1, rows):
            first = jnp.where(lane == r, lane_roll(west[r, :1], r), first)
        count = rows * halves
        left.append(
            jnp.concatenate([east.reshape(count, SUBS, LANES), s_low * first], axis=0)
        )
        right.append(jnp.concatenate([west_next.reshape(count, SUBS, LANES), first], axis=0))
    flux = riemann_flux(left, right, 2)
    low, high = [], []
    for f in range(FIELDS):
        upper = flux[f][:-1].reshape(rows, halves, SUBS, LANES)
        faces = flux[f][-1:]
        fill = jnp.stack([lane_roll(faces, -r) for r in range(rows)], axis=0)
        low.append(from_below(upper, fill))
        high.append(upper)
    return advance(cells, low, high)


def line_flux(cells, normal):
    left, right = [], []
    for a in cells:
        inter = interface(a[:, :-3], a[:, 1:-2], a[:, 2:-1], a[:, 3:])
        west, east = edge_pair(a[:, 2:-2], inter[:, :-1], inter[:, 1:])
        left.append(east[:, :-1])
        right.append(west[:, 1:])
    return riemann_flux(left, right, normal)


def kernel(
    sizes,
    flags_in,
    dens_in,
    press_in,
    vel_in,
    dens_out,
    press_out,
    vel_out,
    flags,
    held,
    ypad,
    zpad,
    done,
    flag_sem,
    in_sem,
    y_send,
    y_recv,
    z_send,
    z_recv,
    out_sem,
):
    planes, rows, halves = sizes
    cells = planes * rows
    step = FIELDS * SUBS
    row, row_count = lax.axis_index("row"), lax.axis_size("row")
    gz, gz_count = lax.axis_index("gz"), lax.axis_size("gz")

    def view(dens, press, vel, f, h):
        ref = (dens, press, vel, vel, vel)[f]
        start = max(f - 2, 0) * cells
        return ref.at[pl.ds(start, cells), pl.ds(h * LANES, LANES)]

    loads = [
        pltpu.make_async_copy(
            view(dens_in, press_in, vel_in, f, h), held.at[f, h], in_sem.at[f, h]
        )
        for f in range(FIELDS)
        for h in range(halves)
    ]
    loads.append(pltpu.make_async_copy(flags_in, flags, flag_sem))
    for copy in loads:
        copy.start()

    barrier = pltpu.get_barrier_semaphore()
    sides = (
        (row > 0, {"row": row - 1}),
        (row < row_count - 1, {"row": row + 1}),
        (gz > 0, {"gz": gz - 1}),
        (gz < gz_count - 1, {"gz": gz + 1}),
    )
    for there, device in sides:

        @pl.when(there)
        def _(device=device):
            pl.semaphore_signal(
                barrier, inc=1, device_id=device, device_id_type=pl.DeviceIdType.MESH
            )

    for copy in loads:
        copy.wait()

    signs = [jnp.where(flags[k] == 1, -1.0, 1.0).astype(jnp.float32) for k in range(6)]

    def swept_rows(which):
        here = [
            jnp.stack(
                [
                    jnp.stack(
                        [held[f, h, pl.ds(r, SUBS, stride=rows), :] for h in range(halves)],
                        axis=0,
                    )
                    for r in which
                ],
                axis=0,
            )
            for f in range(FIELDS)
        ]
        new = x_sweep(here, signs[0], signs[1])
        for f in range(FIELDS):
            for i, r in enumerate(which):
                for h in range(halves):
                    ypad[h, 3 + r, f] = new[f][i, h]

    def y_copy(up, h):
        source, target = (rows, 0) if up else (3, rows + 3)
        return pltpu.make_async_remote_copy(
            src_ref=ypad.at[h, pl.ds(source, 3)],
            dst_ref=ypad.at[h, pl.ds(target, 3)],
            send_sem=y_send.at[up, h],
            recv_sem=y_recv.at[up, h],
            device_id={"row": row + (1 if up else -1)},
            device_id_type=pl.DeviceIdType.MESH,
        )

    def z_copy(up, h):
        source, target = (planes, 0) if up else (3, planes + 3)
        return pltpu.make_async_remote_copy(
            src_ref=zpad.at[h, pl.ds(source * step, 3 * step)],
            dst_ref=zpad.at[h, pl.ds(target * step, 3 * step)],
            send_sem=z_send.at[up, h],
            recv_sem=z_recv.at[up, h],
            device_id={"gz": gz + (1 if up else -1)},
            device_id_type=pl.DeviceIdType.MESH,
        )

    row_up, row_down = row < row_count - 1, row > 0
    gz_up, gz_down = gz < gz_count - 1, gz > 0

    swept_rows(list(range(rows - 3, rows)))
    pl.semaphore_wait(barrier, sum(there.astype(jnp.int32) for there, _ in sides))

    @pl.when(row_up)
    def _():
        for h in range(halves):
            y_copy(1, h).start()

    swept_rows([0, 1, 2])

    @pl.when(row_down)
    def _():
        for h in range(halves):
            y_copy(0, h).start()

    swept_rows(list(range(3, rows - 3)))

    def ghosts(get, put, count, normal, sign, upper):
        for f in range(FIELDS):
            for k in (1, 2, 3):
                inside = count + 3 - k if upper else 2 + k
                edge = count + 2 if upper else 3
                outside = count + 2 + k if upper else 3 - k
                mirror = get(inside, f)
                if f == normal:
                    mirror = -mirror
                put(outside, f, jnp.where(sign < 0.0, mirror, get(edge, f)))

    def y_get(h, j, f):
        return ypad[h, j, f]

    def y_put(h, j, f, value):
        ypad[h, j, f] = value

    def z_get(h, j, f):
        return zpad[h, pl.ds(j * step + f * SUBS, SUBS), :]

    def z_put(h, j, f, value):
        zpad[h, pl.ds(j * step + f * SUBS, SUBS), :] = value

    def swept_line(get, count, normal, arrived, finish):
        def block(h, start, stop):
            return [
                jnp.stack([get(h, j, f) for j in range(start, stop)], axis=0)
                for f in range(FIELDS)
            ]

        blocks = [block(h, 3, count + 3) for h in range(halves)]
        inner = line_flux([jnp.stack(a, axis=0) for a in zip(*blocks)], normal)
        for h in range(halves):
            arrived(h)
            ends = [block(h, 0, 8), block(h, count - 2, count + 6)]
            outer = line_flux([jnp.stack(a, axis=0) for a in zip(*ends)], normal)
            faces = [
                jnp.concatenate([o[0], i[h], o[1]], axis=0) for o, i in zip(outer, inner)
            ]
            new = advance(
                block(h, 3, count + 3), [a[:-1] for a in faces], [a[1:] for a in faces]
            )
            finish(h, new)

    def arrival(copy, get, put, down, up, count, normal, sign_low, sign_high, h):
        @pl.when(down)
        def _():
            copy(1, h).wait_recv()

        @pl.when(jnp.logical_not(down))
        def _():
            ghosts(
                functools.partial(get, h),
                functools.partial(put, h),
                count,
                normal,
                sign_low,
                False,
            )

        @pl.when(up)
        def _():
            copy(0, h).wait_recv()

        @pl.when(jnp.logical_not(up))
        def _():
            ghosts(
                functools.partial(get, h),
                functools.partial(put, h),
                count,
                normal,
                sign_high,
                True,
            )

    def y_finish(h, new):
        for f in range(FIELDS):
            for r in range(rows):
                zpad[h, pl.ds(3 * step + f * SUBS + r, planes, stride=step), :] = new[f][r]

        @pl.when(gz_up)
        def _():
            z_copy(1, h).start()

        @pl.when(gz_down)
        def _():
            z_copy(0, h).start()

    swept_line(
        y_get,
        rows,
        3,
        functools.partial(
            arrival, y_copy, y_get, y_put, row_down, row_up, rows, 3, signs[2], signs[3]
        ),
        y_finish,
    )

    def out_copy(f, h):
        return pltpu.make_async_copy(
            done.at[f, h], view(dens_out, press_out, vel_out, f, h), out_sem.at[f, h]
        )

    def z_finish(h, new):
        for f in range(FIELDS):
            done[f, h] = new[f].reshape(cells, LANES)
            out_copy(f, h).start()

    swept_line(
        z_get,
        planes,
        4,
        functools.partial(
            arrival, z_copy, z_get, z_put, gz_down, gz_up, planes, 4, signs[4], signs[5]
        ),
        z_finish,
    )

    for there, copy, up in (
        (row_up, y_copy, 1),
        (row_down, y_copy, 0),
        (gz_up, z_copy, 1),
        (gz_down, z_copy, 0),
    ):

        @pl.when(there)
        def _(copy=copy, up=up):
            for h in range(halves):
                copy(up, h).wait_send()

    for f in range(FIELDS):
        for h in range(halves):
            out_copy(f, h).wait()


def on_device(density, pressure, velocity, boundary):
    planes, rows, width = density.shape
    cells, halves = planes * rows, width // LANES
    scalar = jax.ShapeDtypeStruct((cells, width), jnp.float32)
    vector = jax.ShapeDtypeStruct((3 * cells, width), jnp.float32)
    anywhere = pl.BlockSpec(memory_space=pltpu.HBM)
    dens, press, vel = pl.pallas_call(
        functools.partial(kernel, (planes, rows, halves)),
        out_shape=(scalar, scalar, vector),
        in_specs=[anywhere] * 4,
        out_specs=(anywhere, anywhere, anywhere),
        scratch_shapes=[
            pltpu.SMEM((6,), jnp.int32),
            pltpu.VMEM((FIELDS, halves, cells, LANES), jnp.float32),
            pltpu.VMEM((halves, rows + 6, FIELDS, planes, LANES), jnp.float32),
            pltpu.VMEM((halves, (planes + 6) * FIELDS * rows, LANES), jnp.float32),
            pltpu.VMEM((FIELDS, halves, cells, LANES), jnp.float32),
            pltpu.SemaphoreType.DMA(()),
            pltpu.SemaphoreType.DMA((FIELDS, halves)),
            pltpu.SemaphoreType.DMA((2, halves)),
            pltpu.SemaphoreType.DMA((2, halves)),
            pltpu.SemaphoreType.DMA((2, halves)),
            pltpu.SemaphoreType.DMA((2, halves)),
            pltpu.SemaphoreType.DMA((FIELDS, halves)),
        ],
        compiler_params=pltpu.CompilerParams(
            collective_id=0, has_side_effects=True, vmem_limit_bytes=64 * 1024 * 1024 - 256 * 1024
        ),
    )(
        boundary,
        density.reshape(cells, width),
        pressure.reshape(cells, width),
        velocity.reshape(3 * cells, width),
    )
    return (
        dens.reshape(planes, rows, width),
        press.reshape(planes, rows, width),
        vel.reshape(3, planes, rows, width),
    )


def solution(mesh):
    in_specs = (P("gz", "row", None), P("gz", "row", None), P(None, "gz", "row", None), P())
    out_specs = (P("gz", "row", None), P("gz", "row", None), P(None, "gz", "row", None))
    return jax.shard_map(
        on_device, mesh=mesh, in_specs=in_specs, out_specs=out_specs, check_vma=False
    )
```

```python
import functools

import jax
import jax.numpy as jnp
from jax import lax
from jax.experimental import pallas as pl
from jax.experimental.pallas import tpu as pltpu
from jax.sharding import PartitionSpec as P

RIEMANN_ITERS = 4
GAMMA = 1.4
COURANT = 0.05
DENS_FLOOR = 0.02
PRESS_FLOOR = 0.02
STAR_FRAC = 0.1
RATIO = (GAMMA + 1.0) / (2.0 * GAMMA)
LANES = 128
SUBS = 8
FIELDS = 5
LIMIT = 62 * 1024 * 1024


def rough_inverse(x):
    return pl.reciprocal(x, approx=True)


def inverse(x):
    y = rough_inverse(x)
    return y * (2.0 - x * y)


def clip_between(x, a, b):
    return jnp.minimum(jnp.maximum(x, jnp.minimum(a, b)), jnp.maximum(a, b))


def edge_pair(centre, lower, upper):
    dl = lower - centre
    dr = upper - centre
    rl = 2.0 * jnp.abs(dl)
    rr = 2.0 * jnp.abs(dr)
    west = centre + jnp.minimum(jnp.maximum(dl, -rr), rr)
    east = centre + jnp.minimum(jnp.maximum(dr, -rl), rl)
    return west, east


def interface(far_left, left, right, far_right):
    value = (7.0 * (left + right) - (far_left + far_right)) * (1.0 / 12.0)
    return clip_between(value, left, right)


def riemann_flux(left, right, normal):
    rho_l, p_l, u_l = left[0], left[1], left[normal]
    rho_r, p_r, u_r = right[0], right[1], right[normal]
    inv_c_l = lax.rsqrt(GAMMA * p_l * rho_l)
    inv_c_r = lax.rsqrt(GAMMA * p_r * rho_r)
    slope_l = RATIO * inverse(p_l)
    slope_r = RATIO * inverse(p_r)
    du = u_r - u_l
    floor = STAR_FRAC * jnp.minimum(p_l, p_r)
    star = (p_l * inv_c_l + p_r * inv_c_r - du) * inverse(inv_c_l + inv_c_r)
    star = jnp.maximum(star, floor)

    def jump(star, p, inv_c, slope):
        r = lax.rsqrt((1.0 - RATIO) + slope * star)
        t = inv_c * r
        return (star - p) * t, r, t

    for _ in range(RIEMANN_ITERS):
        f_l, r_l, t_l = jump(star, p_l, inv_c_l, slope_l)
        f_r, r_r, t_r = jump(star, p_r, inv_c_r, slope_r)
        twice = t_l * (1.0 + r_l * r_l) + t_r * (1.0 + r_r * r_r)
        total = du + f_l + f_r
        star = star - (total + total) * rough_inverse(twice)
        star = jnp.maximum(star, floor)
    f_l, _, _ = jump(star, p_l, inv_c_l, slope_l)
    f_r, _, _ = jump(star, p_r, inv_c_r, slope_r)
    speed = 0.5 * ((u_l - f_l) + (u_r + f_r))
    up = speed > 0.0
    vel = [speed if a == normal else jnp.where(up, left[a], right[a]) for a in (2, 3, 4)]
    rho = jnp.where(up, rho_l, rho_r)
    press = jnp.where(up, p_l, p_r)
    energy = press * (1.0 / (GAMMA - 1.0)) + 0.5 * rho * (
        vel[0] * vel[0] + vel[1] * vel[1] + vel[2] * vel[2]
    )
    mass = rho * speed
    flux = [mass, (energy + star) * speed] + [mass * v for v in vel]
    flux[normal] = flux[normal] + star
    return flux


def advance(cells, low, high):
    rho, press = cells[0], cells[1]
    vel = cells[2:5]
    energy = press * (1.0 / (GAMMA - 1.0)) + 0.5 * rho * (
        vel[0] * vel[0] + vel[1] * vel[1] + vel[2] * vel[2]
    )
    old = [rho, energy] + [rho * v for v in vel]
    new = [o - COURANT * (h - l) for o, h, l in zip(old, high, low)]
    rho = jnp.maximum(new[0], DENS_FLOOR)
    inv = inverse(rho)
    vel = [m * inv for m in new[2:5]]
    press = (GAMMA - 1.0) * (
        new[1] - 0.5 * rho * (vel[0] * vel[0] + vel[1] * vel[1] + vel[2] * vel[2])
    )
    return [rho, jnp.maximum(press, PRESS_FLOOR)] + vel


def lane_roll(a, shift):
    if shift % LANES == 0:
        return a
    flat = a.reshape(-1, LANES)
    return pltpu.roll(flat, shift % LANES, 1).reshape(a.shape)


def from_below(a, fill):
    lane = lax.broadcasted_iota(jnp.int32, a.shape, 3)
    rolled = lane_roll(a, 1)
    other = jnp.concatenate([fill, rolled[:, :-1]], axis=1)
    return jnp.where(lane == 0, other, rolled)


def from_above(a, fill):
    lane = lax.broadcasted_iota(jnp.int32, a.shape, 3)
    rolled = lane_roll(a, LANES - 1)
    other = jnp.concatenate([rolled[:, 1:], fill], axis=1)
    return jnp.where(lane == LANES - 1, other, rolled)


def x_sweep(cells, sign_low, sign_high):
    rows, halves = cells[0].shape[:2]
    lane = lax.broadcasted_iota(jnp.int32, (1, SUBS, LANES), 2)
    left, right = [], []
    for f, a in enumerate(cells):
        s_low = sign_low if f == 2 else 1.0
        s_high = sign_high if f == 2 else 1.0
        below = from_below(a, s_low * a[:, :1])
        above = from_above(a, s_high * a[:, -1:])
        above2 = from_above(above, s_high * below[:, -1:])
        upper = interface(below, a, above, above2)
        lower = from_below(upper, 0.5 * (a[:, :1] + s_low * a[:, :1]))
        west, east = edge_pair(a, lower, upper)
        west_next = from_above(west, s_high * east[:, -1:])
        first = west[0, :1]
        for r in range(1, rows):
            first = jnp.where(lane == r, lane_roll(west[r, :1], r), first)
        count = rows * halves
        left.append(
            jnp.concatenate([east.reshape(count, SUBS, LANES), s_low * first], axis=0)
        )
        right.append(jnp.concatenate([west_next.reshape(count, SUBS, LANES), first], axis=0))
    flux = riemann_flux(left, right, 2)
    low, high = [], []
    for f in range(FIELDS):
        upper = flux[f][:-1].reshape(rows, halves, SUBS, LANES)
        faces = flux[f][-1:]
        fill = jnp.stack([lane_roll(faces, -r) for r in range(rows)], axis=0)
        low.append(from_below(upper, fill))
        high.append(upper)
    return advance(cells, low, high)


def line_flux(cells, normal):
    left, right = [], []
    for a in cells:
        inter = interface(a[:, :-3], a[:, 1:-2], a[:, 2:-1], a[:, 3:])
        west, east = edge_pair(a[:, 2:-2], inter[:, :-1], inter[:, 1:])
        left.append(east[:, :-1])
        right.append(west[:, 1:])
    return riemann_flux(left, right, normal)


def view(refs, cells, f, h):
    start = max(f - 2, 0) * cells
    return refs[min(f, 2)].at[pl.ds(start, cells), pl.ds(h * LANES, LANES)]


def block(get, h, start, stop):
    return [
        jnp.stack([get(h, j, f) for j in range(start, stop)], axis=0) for f in range(FIELDS)
    ]


def z_tile(zpad, h, j, f):
    return zpad[h, pl.ds((j * FIELDS + f) * SUBS, SUBS), :]


def inner_faces(get, halves, count, normal):
    blocks = [block(get, h, 3, count + 3) for h in range(halves)]
    return line_flux([jnp.stack(a, axis=0) for a in zip(*blocks)], normal)


def finished(get, h, count, normal, inner):
    ends = [block(get, h, 0, 8), block(get, h, count - 2, count + 6)]
    outer = line_flux([jnp.stack(a, axis=0) for a in zip(*ends)], normal)
    faces = [jnp.concatenate([o[0], i, o[1]], axis=0) for o, i in zip(outer, inner)]
    own = block(get, h, 3, count + 3)
    return advance(own, [a[:-1] for a in faces], [a[1:] for a in faces])


def last_kernel(sizes, zpad, inner, done, dens_out, press_out, vel_out, mine, out_sem):
    planes, rows, halves = sizes
    cells, last = planes * rows, halves - 1

    def out_copy(f, h):
        return pltpu.make_async_copy(
            mine.at[f] if h == last else done.at[f, h],
            view((dens_out, press_out, vel_out), cells, f, h),
            out_sem.at[f, h],
        )

    for h in range(last):
        for f in range(FIELDS):
            out_copy(f, h).start()
    new = finished(
        functools.partial(z_tile, zpad), last, planes, 4, [inner[f] for f in range(FIELDS)]
    )
    for f in range(FIELDS):
        mine[f] = new[f].reshape(cells, LANES)
        out_copy(f, last).start()
    for h in range(halves):
        for f in range(FIELDS):
            out_copy(f, h).wait()


def kernel(
    sizes,
    flags_in,
    dens_in,
    press_in,
    vel_in,
    zpad,
    inner_out,
    done,
    flags,
    held,
    ypad,
    flag_sem,
    in_sem,
    y_send,
    y_recv,
    z_send,
    z_recv,
):
    planes, rows, halves = sizes
    cells = planes * rows
    step = FIELDS * SUBS
    row, row_count = lax.axis_index("row"), lax.axis_size("row")
    gz, gz_count = lax.axis_index("gz"), lax.axis_size("gz")

    loads = [
        pltpu.make_async_copy(
            view((dens_in, press_in, vel_in), cells, f, h), held.at[f, h], in_sem.at[f, h]
        )
        for f in range(FIELDS)
        for h in range(halves)
    ]
    loads.append(pltpu.make_async_copy(flags_in, flags, flag_sem))
    for copy in loads:
        copy.start()

    barrier = pltpu.get_barrier_semaphore()
    sides = (
        (row > 0, {"row": row - 1}),
        (row < row_count - 1, {"row": row + 1}),
        (gz > 0, {"gz": gz - 1}),
        (gz < gz_count - 1, {"gz": gz + 1}),
    )
    for there, device in sides:

        @pl.when(there)
        def _(device=device):
            pl.semaphore_signal(
                barrier, inc=1, device_id=device, device_id_type=pl.DeviceIdType.MESH
            )

    for copy in loads:
        copy.wait()

    signs = [jnp.where(flags[k] == 1, -1.0, 1.0).astype(jnp.float32) for k in range(6)]

    def swept_rows(which):
        here = [
            jnp.stack(
                [
                    jnp.stack(
                        [held[f, h, pl.ds(r, SUBS, stride=rows), :] for h in range(halves)],
                        axis=0,
                    )
                    for r in which
                ],
                axis=0,
            )
            for f in range(FIELDS)
        ]
        new = x_sweep(here, signs[0], signs[1])
        for f in range(FIELDS):
            for i, r in enumerate(which):
                for h in range(halves):
                    ypad[h, 3 + r, f] = new[f][i, h]

    def y_copy(up, h):
        source, target = (rows, 0) if up else (3, rows + 3)
        return pltpu.make_async_remote_copy(
            src_ref=ypad.at[h, pl.ds(source, 3)],
            dst_ref=ypad.at[h, pl.ds(target, 3)],
            send_sem=y_send.at[up, h],
            recv_sem=y_recv.at[up, h],
            device_id={"row": row + (1 if up else -1)},
            device_id_type=pl.DeviceIdType.MESH,
        )

    def z_copy(up, h):
        source, target = (planes, 0) if up else (3, planes + 3)
        return pltpu.make_async_remote_copy(
            src_ref=zpad.at[h, pl.ds(source * step, 3 * step)],
            dst_ref=zpad.at[h, pl.ds(target * step, 3 * step)],
            send_sem=z_send.at[up, h],
            recv_sem=z_recv.at[up, h],
            device_id={"gz": gz + (1 if up else -1)},
            device_id_type=pl.DeviceIdType.MESH,
        )

    row_up, row_down = row < row_count - 1, row > 0
    gz_up, gz_down = gz < gz_count - 1, gz > 0

    swept_rows(list(range(rows - 3, rows)))
    pl.semaphore_wait(barrier, sum(there.astype(jnp.int32) for there, _ in sides))

    @pl.when(row_up)
    def _():
        for h in range(halves):
            y_copy(1, h).start()

    swept_rows([0, 1, 2])

    @pl.when(row_down)
    def _():
        for h in range(halves):
            y_copy(0, h).start()

    swept_rows(list(range(3, rows - 3)))

    def ghosts(get, put, count, normal, sign, upper):
        for f in range(FIELDS):
            for k in (1, 2, 3):
                inside = count + 3 - k if upper else 2 + k
                edge = count + 2 if upper else 3
                outside = count + 2 + k if upper else 3 - k
                mirror = get(inside, f)
                if f == normal:
                    mirror = -mirror
                put(outside, f, jnp.where(sign < 0.0, mirror, get(edge, f)))

    def y_get(h, j, f):
        return ypad[h, j, f]

    def y_put(h, j, f, value):
        ypad[h, j, f] = value

    z_get = functools.partial(z_tile, zpad)

    def z_put(h, j, f, value):
        zpad[h, pl.ds(j * step + f * SUBS, SUBS), :] = value

    def arrival(copy, get, put, down, up, count, normal, sign_low, sign_high, h):
        @pl.when(down)
        def _():
            copy(1, h).wait_recv()

        @pl.when(jnp.logical_not(down))
        def _():
            ghosts(
                functools.partial(get, h),
                functools.partial(put, h),
                count,
                normal,
                sign_low,
                False,
            )

        @pl.when(up)
        def _():
            copy(0, h).wait_recv()

        @pl.when(jnp.logical_not(up))
        def _():
            ghosts(
                functools.partial(get, h),
                functools.partial(put, h),
                count,
                normal,
                sign_high,
                True,
            )

    def y_finish(h, new):
        for f in range(FIELDS):
            for r in range(rows):
                zpad[h, pl.ds(3 * step + f * SUBS + r, planes, stride=step), :] = new[f][r]

        @pl.when(gz_up)
        def _():
            z_copy(1, h).start()

        @pl.when(gz_down)
        def _():
            z_copy(0, h).start()

    inner = inner_faces(y_get, halves, rows, 3)
    for h in range(halves):
        arrival(y_copy, y_get, y_put, row_down, row_up, rows, 3, signs[2], signs[3], h)
        y_finish(h, finished(y_get, h, rows, 3, [i[h] for i in inner]))

    inner = inner_faces(z_get, halves, planes, 4)
    for f in range(FIELDS):
        inner_out[f] = inner[f][halves - 1]
    for h in range(halves):
        arrival(z_copy, z_get, z_put, gz_down, gz_up, planes, 4, signs[4], signs[5], h)
        if h < halves - 1:
            new = finished(z_get, h, planes, 4, [i[h] for i in inner])
            for f in range(FIELDS):
                done[f, h] = new[f].reshape(cells, LANES)

    for there, copy, up in (
        (row_up, y_copy, 1),
        (row_down, y_copy, 0),
        (gz_up, z_copy, 1),
        (gz_down, z_copy, 0),
    ):

        @pl.when(there)
        def _(copy=copy, up=up):
            for h in range(halves):
                copy(up, h).wait_send()


def on_device(density, pressure, velocity, boundary):
    planes, rows, width = density.shape
    cells, halves = planes * rows, width // LANES
    sizes = (planes, rows, halves)
    scalar = pltpu.HBM((cells, width), jnp.float32)
    vector = pltpu.HBM((3 * cells, width), jnp.float32)
    hbm = pl.BlockSpec(memory_space=pltpu.HBM)
    vmem = pl.BlockSpec(memory_space=pltpu.VMEM)
    between = pl.pallas_call(
        functools.partial(kernel, sizes),
        out_shape=(
            pltpu.VMEM((halves, (planes + 6) * FIELDS * rows, LANES), jnp.float32),
            pltpu.VMEM((FIELDS, planes - 5, rows, LANES), jnp.float32),
            pltpu.VMEM((FIELDS, halves - 1, cells, LANES), jnp.float32),
        ),
        in_specs=[hbm] * 4,
        out_specs=(vmem, vmem, vmem),
        scratch_shapes=[
            pltpu.SMEM((6,), jnp.int32),
            pltpu.VMEM((FIELDS, halves, cells, LANES), jnp.float32),
            pltpu.VMEM((halves, rows + 6, FIELDS, planes, LANES), jnp.float32),
            pltpu.SemaphoreType.DMA(()),
            pltpu.SemaphoreType.DMA((FIELDS, halves)),
            pltpu.SemaphoreType.DMA((2, halves)),
            pltpu.SemaphoreType.DMA((2, halves)),
            pltpu.SemaphoreType.DMA((2, halves)),
            pltpu.SemaphoreType.DMA((2, halves)),
        ],
        compiler_params=pltpu.CompilerParams(
            collective_id=0, has_side_effects=True, vmem_limit_bytes=LIMIT
        ),
    )(
        boundary,
        density.reshape(cells, width),
        pressure.reshape(cells, width),
        velocity.reshape(3 * cells, width),
    )
    dens, press, vel = pl.pallas_call(
        functools.partial(last_kernel, sizes),
        out_shape=(scalar, scalar, vector),
        in_specs=[vmem] * 3,
        out_specs=(hbm, hbm, hbm),
        scratch_shapes=[
            pltpu.VMEM((FIELDS, cells, LANES), jnp.float32),
            pltpu.SemaphoreType.DMA((FIELDS, halves)),
        ],
        compiler_params=pltpu.CompilerParams(vmem_limit_bytes=16 * 1024 * 1024),
    )(*between)
    return (
        dens.reshape(planes, rows, width),
        press.reshape(planes, rows, width),
        vel.reshape(3, planes, rows, width),
    )


def solution(mesh):
    in_specs = (P("gz", "row", None), P("gz", "row", None), P(None, "gz", "row", None), P())
    out_specs = (P("gz", "row", None), P("gz", "row", None), P(None, "gz", "row", None))
    return jax.shard_map(
        on_device, mesh=mesh, in_specs=in_specs, out_specs=out_specs, check_vma=False
    )
```

```python
import functools

import jax
import jax.numpy as jnp
from jax import lax
from jax.experimental import pallas as pl
from jax.experimental.pallas import tpu as pltpu
from jax.sharding import PartitionSpec as P

RIEMANN_ITERS = 4
GAMMA = 1.4
COURANT = 0.05
DENS_FLOOR = 0.02
PRESS_FLOOR = 0.02
STAR_FRAC = 0.1
RATIO = (GAMMA + 1.0) / (2.0 * GAMMA)
LANES = 128
SUBS = 8
FIELDS = 5
LIMIT = 62 * 1024 * 1024


def rough_inverse(x):
    return pl.reciprocal(x, approx=True)


def inverse(x):
    y = rough_inverse(x)
    return y * (2.0 - x * y)


def clip_between(x, a, b):
    return jnp.minimum(jnp.maximum(x, jnp.minimum(a, b)), jnp.maximum(a, b))


def edge_pair(centre, lower, upper):
    dl = lower - centre
    dr = upper - centre
    rl = 2.0 * jnp.abs(dl)
    rr = 2.0 * jnp.abs(dr)
    west = centre + jnp.minimum(jnp.maximum(dl, -rr), rr)
    east = centre + jnp.minimum(jnp.maximum(dr, -rl), rl)
    return west, east


def interface(far_left, left, right, far_right):
    value = (7.0 * (left + right) - (far_left + far_right)) * (1.0 / 12.0)
    return clip_between(value, left, right)


def riemann_flux(left, right, normal):
    rho_l, p_l, u_l = left[0], left[1], left[normal]
    rho_r, p_r, u_r = right[0], right[1], right[normal]
    inv_c_l = lax.rsqrt(GAMMA * p_l * rho_l)
    inv_c_r = lax.rsqrt(GAMMA * p_r * rho_r)
    slope_l = RATIO * inverse(p_l)
    slope_r = RATIO * inverse(p_r)
    du = u_r - u_l
    floor = STAR_FRAC * jnp.minimum(p_l, p_r)
    star = (p_l * inv_c_l + p_r * inv_c_r - du) * rough_inverse(inv_c_l + inv_c_r)
    star = jnp.maximum(star, floor)

    def jump(star, p, inv_c, slope):
        r = lax.rsqrt((1.0 - RATIO) + slope * star)
        t = inv_c * r
        return (star - p) * t, r, t

    for _ in range(RIEMANN_ITERS):
        f_l, r_l, t_l = jump(star, p_l, inv_c_l, slope_l)
        f_r, r_r, t_r = jump(star, p_r, inv_c_r, slope_r)
        twice = t_l * (1.0 + r_l * r_l) + t_r * (1.0 + r_r * r_r)
        total = du + f_l + f_r
        star = star - (total + total) * rough_inverse(twice)
        star = jnp.maximum(star, floor)
    f_l, _, _ = jump(star, p_l, inv_c_l, slope_l)
    f_r, _, _ = jump(star, p_r, inv_c_r, slope_r)
    speed = 0.5 * ((u_l - f_l) + (u_r + f_r))
    up = speed > 0.0
    vel = [speed if a == normal else jnp.where(up, left[a], right[a]) for a in (2, 3, 4)]
    rho = jnp.where(up, rho_l, rho_r)
    press = jnp.where(up, p_l, p_r)
    energy = press * (1.0 / (GAMMA - 1.0)) + 0.5 * rho * (
        vel[0] * vel[0] + vel[1] * vel[1] + vel[2] * vel[2]
    )
    mass = rho * speed
    flux = [mass, (energy + star) * speed] + [mass * v for v in vel]
    flux[normal] = flux[normal] + star
    return flux


def advance(cells, low, high):
    rho, press = cells[0], cells[1]
    vel = cells[2:5]
    energy = press * (1.0 / (GAMMA - 1.0)) + 0.5 * rho * (
        vel[0] * vel[0] + vel[1] * vel[1] + vel[2] * vel[2]
    )
    old = [rho, energy] + [rho * v for v in vel]
    new = [o - COURANT * (h - l) for o, h, l in zip(old, high, low)]
    rho = jnp.maximum(new[0], DENS_FLOOR)
    inv = inverse(rho)
    vel = [m * inv for m in new[2:5]]
    press = (GAMMA - 1.0) * (
        new[1] - 0.5 * rho * (vel[0] * vel[0] + vel[1] * vel[1] + vel[2] * vel[2])
    )
    return [rho, jnp.maximum(press, PRESS_FLOOR)] + vel


def lane_roll(a, shift):
    if shift % LANES == 0:
        return a
    flat = a.reshape(-1, LANES)
    return pltpu.roll(flat, shift % LANES, 1).reshape(a.shape)


def from_below(a, fill):
    lane = lax.broadcasted_iota(jnp.int32, a.shape, 3)
    rolled = lane_roll(a, 1)
    other = jnp.concatenate([fill, rolled[:, :-1]], axis=1)
    return jnp.where(lane == 0, other, rolled)


def from_above(a, fill):
    lane = lax.broadcasted_iota(jnp.int32, a.shape, 3)
    rolled = lane_roll(a, LANES - 1)
    other = jnp.concatenate([rolled[:, 1:], fill], axis=1)
    return jnp.where(lane == LANES - 1, other, rolled)


def x_sweep(cells, sign_low, sign_high):
    rows, halves = cells[0].shape[:2]
    lane = lax.broadcasted_iota(jnp.int32, (1, SUBS, LANES), 2)
    left, right = [], []
    for f, a in enumerate(cells):
        s_low = sign_low if f == 2 else 1.0
        s_high = sign_high if f == 2 else 1.0
        below = from_below(a, s_low * a[:, :1])
        above = from_above(a, s_high * a[:, -1:])
        above2 = from_above(above, s_high * below[:, -1:])
        upper = interface(below, a, above, above2)
        lower = from_below(upper, 0.5 * (a[:, :1] + s_low * a[:, :1]))
        west, east = edge_pair(a, lower, upper)
        west_next = from_above(west, s_high * east[:, -1:])
        first = west[0, :1]
        for r in range(1, rows):
            first = jnp.where(lane == r, lane_roll(west[r, :1], r), first)
        count = rows * halves
        left.append(
            jnp.concatenate([east.reshape(count, SUBS, LANES), s_low * first], axis=0)
        )
        right.append(jnp.concatenate([west_next.reshape(count, SUBS, LANES), first], axis=0))
    flux = riemann_flux(left, right, 2)
    low, high = [], []
    for f in range(FIELDS):
        upper = flux[f][:-1].reshape(rows, halves, SUBS, LANES)
        faces = flux[f][-1:]
        fill = jnp.stack([lane_roll(faces, -r) for r in range(rows)], axis=0)
        low.append(from_below(upper, fill))
        high.append(upper)
    return advance(cells, low, high)


def line_flux(cells, normal):
    left, right = [], []
    for a in cells:
        inter = interface(a[:, :-3], a[:, 1:-2], a[:, 2:-1], a[:, 3:])
        west, east = edge_pair(a[:, 2:-2], inter[:, :-1], inter[:, 1:])
        left.append(east[:, :-1])
        right.append(west[:, 1:])
    return riemann_flux(left, right, normal)


def view(refs, cells, f, h):
    start = max(f - 2, 0) * cells
    return refs[min(f, 2)].at[pl.ds(start, cells), pl.ds(h * LANES, LANES)]


def block(get, h, start, stop):
    return [
        jnp.stack([get(h, j, f) for j in range(start, stop)], axis=0) for f in range(FIELDS)
    ]


def z_tile(zpad, h, j, f):
    return zpad[h, pl.ds((j * FIELDS + f) * SUBS, SUBS), :]


def inner_faces(get, halves, count, normal):
    blocks = [block(get, h, 3, count + 3) for h in range(halves)]
    return line_flux([jnp.stack(a, axis=0) for a in zip(*blocks)], normal)


def finished(get, h, count, normal, inner):
    ends = [block(get, h, 0, 8), block(get, h, count - 2, count + 6)]
    outer = line_flux([jnp.stack(a, axis=0) for a in zip(*ends)], normal)
    faces = [jnp.concatenate([o[0], i, o[1]], axis=0) for o, i in zip(outer, inner)]
    own = block(get, h, 3, count + 3)
    return advance(own, [a[:-1] for a in faces], [a[1:] for a in faces])


def last_kernel(sizes, zpad, inner, done, dens_out, press_out, vel_out, mine, out_sem):
    planes, rows, halves = sizes
    cells, last = planes * rows, halves - 1

    def out_copy(f, h):
        return pltpu.make_async_copy(
            mine.at[f] if h == last else done.at[f, h],
            view((dens_out, press_out, vel_out), cells, f, h),
            out_sem.at[f, h],
        )

    for h in range(last):
        for f in range(FIELDS):
            out_copy(f, h).start()
    new = finished(
        functools.partial(z_tile, zpad), last, planes, 4, [inner[f] for f in range(FIELDS)]
    )
    for f in range(FIELDS):
        mine[f] = new[f].reshape(cells, LANES)
        out_copy(f, last).start()
    for h in range(halves):
        for f in range(FIELDS):
            out_copy(f, h).wait()


def kernel(
    sizes,
    flags_in,
    dens_in,
    press_in,
    vel_in,
    zpad,
    inner_out,
    done,
    flags,
    held,
    ypad,
    flag_sem,
    in_sem,
    y_send,
    y_recv,
    z_send,
    z_recv,
):
    planes, rows, halves = sizes
    cells = planes * rows
    step = FIELDS * SUBS
    row, row_count = lax.axis_index("row"), lax.axis_size("row")
    gz, gz_count = lax.axis_index("gz"), lax.axis_size("gz")

    loads = [
        pltpu.make_async_copy(
            view((dens_in, press_in, vel_in), cells, f, h), held.at[f, h], in_sem.at[f, h]
        )
        for f in range(FIELDS)
        for h in range(halves)
    ]
    loads.append(pltpu.make_async_copy(flags_in, flags, flag_sem))
    for copy in loads:
        copy.start()

    barrier = pltpu.get_barrier_semaphore()
    sides = (
        (row > 0, {"row": row - 1}),
        (row < row_count - 1, {"row": row + 1}),
        (gz > 0, {"gz": gz - 1}),
        (gz < gz_count - 1, {"gz": gz + 1}),
    )
    for there, device in sides:

        @pl.when(there)
        def _(device=device):
            pl.semaphore_signal(
                barrier, inc=1, device_id=device, device_id_type=pl.DeviceIdType.MESH
            )

    for copy in loads:
        copy.wait()

    signs = [jnp.where(flags[k] == 1, -1.0, 1.0).astype(jnp.float32) for k in range(6)]

    def swept_rows(which):
        here = [
            jnp.stack(
                [
                    jnp.stack(
                        [held[f, h, pl.ds(r, SUBS, stride=rows), :] for h in range(halves)],
                        axis=0,
                    )
                    for r in which
                ],
                axis=0,
            )
            for f in range(FIELDS)
        ]
        new = x_sweep(here, signs[0], signs[1])
        for f in range(FIELDS):
            for i, r in enumerate(which):
                for h in range(halves):
                    ypad[h, 3 + r, f] = new[f][i, h]

    def y_copy(up, h):
        source, target = (rows, 0) if up else (3, rows + 3)
        return pltpu.make_async_remote_copy(
            src_ref=ypad.at[h, pl.ds(source, 3)],
            dst_ref=ypad.at[h, pl.ds(target, 3)],
            send_sem=y_send.at[up, h],
            recv_sem=y_recv.at[up, h],
            device_id={"row": row + (1 if up else -1)},
            device_id_type=pl.DeviceIdType.MESH,
        )

    def z_copy(up, h):
        source, target = (planes, 0) if up else (3, planes + 3)
        return pltpu.make_async_remote_copy(
            src_ref=zpad.at[h, pl.ds(source * step, 3 * step)],
            dst_ref=zpad.at[h, pl.ds(target * step, 3 * step)],
            send_sem=z_send.at[up, h],
            recv_sem=z_recv.at[up, h],
            device_id={"gz": gz + (1 if up else -1)},
            device_id_type=pl.DeviceIdType.MESH,
        )

    row_up, row_down = row < row_count - 1, row > 0
    gz_up, gz_down = gz < gz_count - 1, gz > 0

    odd = row % 2 == 1
    first = (row % 2) * (rows - 3)
    second = (rows - 3) - first

    def send_rows(up, when):
        @pl.when(when)
        def _():
            for h in range(halves):
                y_copy(up, h).start()

    swept_rows([first + i for i in range(3)])
    pl.semaphore_wait(barrier, sum(there.astype(jnp.int32) for there, _ in sides))
    send_rows(1, jnp.logical_and(row_up, odd))
    send_rows(0, jnp.logical_and(row_down, jnp.logical_not(odd)))
    swept_rows([second + i for i in range(3)])
    send_rows(1, jnp.logical_and(row_up, jnp.logical_not(odd)))
    send_rows(0, jnp.logical_and(row_down, odd))
    swept_rows(list(range(3, rows - 3)))

    def ghosts(get, put, count, normal, sign, upper):
        for f in range(FIELDS):
            for k in (1, 2, 3):
                inside = count + 3 - k if upper else 2 + k
                edge = count + 2 if upper else 3
                outside = count + 2 + k if upper else 3 - k
                mirror = get(inside, f)
                if f == normal:
                    mirror = -mirror
                put(outside, f, jnp.where(sign < 0.0, mirror, get(edge, f)))

    def y_get(h, j, f):
        return ypad[h, j, f]

    def y_put(h, j, f, value):
        ypad[h, j, f] = value

    z_get = functools.partial(z_tile, zpad)

    def z_put(h, j, f, value):
        zpad[h, pl.ds(j * step + f * SUBS, SUBS), :] = value

    def arrival(copy, get, put, down, up, count, normal, sign_low, sign_high, h):
        @pl.when(down)
        def _():
            copy(1, h).wait_recv()

        @pl.when(jnp.logical_not(down))
        def _():
            ghosts(
                functools.partial(get, h),
                functools.partial(put, h),
                count,
                normal,
                sign_low,
                False,
            )

        @pl.when(up)
        def _():
            copy(0, h).wait_recv()

        @pl.when(jnp.logical_not(up))
        def _():
            ghosts(
                functools.partial(get, h),
                functools.partial(put, h),
                count,
                normal,
                sign_high,
                True,
            )

    def y_finish(h, new):
        for f in range(FIELDS):
            for r in range(rows):
                zpad[h, pl.ds(3 * step + f * SUBS + r, planes, stride=step), :] = new[f][r]

        @pl.when(gz_up)
        def _():
            z_copy(1, h).start()

        @pl.when(gz_down)
        def _():
            z_copy(0, h).start()

    inner = inner_faces(y_get, halves, rows, 3)
    for h in range(halves):
        arrival(y_copy, y_get, y_put, row_down, row_up, rows, 3, signs[2], signs[3], h)
        y_finish(h, finished(y_get, h, rows, 3, [i[h] for i in inner]))

    inner = inner_faces(z_get, halves, planes, 4)
    for f in range(FIELDS):
        inner_out[f] = inner[f][halves - 1]
    for h in range(halves):
        arrival(z_copy, z_get, z_put, gz_down, gz_up, planes, 4, signs[4], signs[5], h)
        if h < halves - 1:
            new = finished(z_get, h, planes, 4, [i[h] for i in inner])
            for f in range(FIELDS):
                done[f, h] = new[f].reshape(cells, LANES)

    for there, copy, up in (
        (row_up, y_copy, 1),
        (row_down, y_copy, 0),
        (gz_up, z_copy, 1),
        (gz_down, z_copy, 0),
    ):

        @pl.when(there)
        def _(copy=copy, up=up):
            for h in range(halves):
                copy(up, h).wait_send()


def on_device(density, pressure, velocity, boundary):
    planes, rows, width = density.shape
    cells, halves = planes * rows, width // LANES
    sizes = (planes, rows, halves)
    scalar = pltpu.HBM((cells, width), jnp.float32)
    vector = pltpu.HBM((3 * cells, width), jnp.float32)
    hbm = pl.BlockSpec(memory_space=pltpu.HBM)
    vmem = pl.BlockSpec(memory_space=pltpu.VMEM)
    between = pl.pallas_call(
        functools.partial(kernel, sizes),
        out_shape=(
            pltpu.VMEM((halves, (planes + 6) * FIELDS * rows, LANES), jnp.float32),
            pltpu.VMEM((FIELDS, planes - 5, rows, LANES), jnp.float32),
            pltpu.VMEM((FIELDS, halves - 1, cells, LANES), jnp.float32),
        ),
        in_specs=[hbm] * 4,
        out_specs=(vmem, vmem, vmem),
        scratch_shapes=[
            pltpu.SMEM((6,), jnp.int32),
            pltpu.VMEM((FIELDS, halves, cells, LANES), jnp.float32),
            pltpu.VMEM((halves, rows + 6, FIELDS, planes, LANES), jnp.float32),
            pltpu.SemaphoreType.DMA(()),
            pltpu.SemaphoreType.DMA((FIELDS, halves)),
            pltpu.SemaphoreType.DMA((2, halves)),
            pltpu.SemaphoreType.DMA((2, halves)),
            pltpu.SemaphoreType.DMA((2, halves)),
            pltpu.SemaphoreType.DMA((2, halves)),
        ],
        compiler_params=pltpu.CompilerParams(
            collective_id=0, has_side_effects=True, vmem_limit_bytes=LIMIT
        ),
    )(
        boundary,
        density.reshape(cells, width),
        pressure.reshape(cells, width),
        velocity.reshape(3 * cells, width),
    )
    dens, press, vel = pl.pallas_call(
        functools.partial(last_kernel, sizes),
        out_shape=(scalar, scalar, vector),
        in_specs=[vmem] * 3,
        out_specs=(hbm, hbm, hbm),
        scratch_shapes=[
            pltpu.VMEM((FIELDS, cells, LANES), jnp.float32),
            pltpu.SemaphoreType.DMA((FIELDS, halves)),
        ],
        compiler_params=pltpu.CompilerParams(vmem_limit_bytes=16 * 1024 * 1024),
    )(*between)
    return (
        dens.reshape(planes, rows, width),
        press.reshape(planes, rows, width),
        vel.reshape(3, planes, rows, width),
    )


def solution(mesh):
    in_specs = (P("gz", "row", None), P("gz", "row", None), P(None, "gz", "row", None), P())
    out_specs = (P("gz", "row", None), P("gz", "row", None), P(None, "gz", "row", None))
    return jax.shard_map(
        on_device, mesh=mesh, in_specs=in_specs, out_specs=out_specs, check_vma=False
    )
```

```python
import functools

import jax
import jax.numpy as jnp
from jax import lax
from jax.experimental import pallas as pl
from jax.experimental.pallas import tpu as pltpu
from jax.sharding import PartitionSpec as P

RIEMANN_ITERS = 4
GAMMA = 1.4
COURANT = 0.05
DENS_FLOOR = 0.02
PRESS_FLOOR = 0.02
STAR_FRAC = 0.1
RATIO = (GAMMA + 1.0) / (2.0 * GAMMA)
LANES = 128
SUBS = 8
FIELDS = 5
LIMIT = 62 * 1024 * 1024


def rough_inverse(x):
    return pl.reciprocal(x, approx=True)


def inverse(x):
    y = rough_inverse(x)
    return y * (2.0 - x * y)


def clip_between(x, a, b):
    return jnp.minimum(jnp.maximum(x, jnp.minimum(a, b)), jnp.maximum(a, b))


def edge_pair(centre, lower, upper):
    dl = lower - centre
    dr = upper - centre
    rl = 2.0 * jnp.abs(dl)
    rr = 2.0 * jnp.abs(dr)
    west = centre + jnp.minimum(jnp.maximum(dl, -rr), rr)
    east = centre + jnp.minimum(jnp.maximum(dr, -rl), rl)
    return west, east


def interface(far_left, left, right, far_right):
    value = (7.0 * (left + right) - (far_left + far_right)) * (1.0 / 12.0)
    return clip_between(value, left, right)


def riemann_flux(left, right, normal):
    rho_l, p_l, u_l = left[0], left[1], left[normal]
    rho_r, p_r, u_r = right[0], right[1], right[normal]
    inv_c_l = lax.rsqrt(GAMMA * p_l * rho_l)
    inv_c_r = lax.rsqrt(GAMMA * p_r * rho_r)
    slope_l = RATIO * inverse(p_l)
    slope_r = RATIO * inverse(p_r)
    du = u_r - u_l
    floor = STAR_FRAC * jnp.minimum(p_l, p_r)
    star = (p_l * inv_c_l + p_r * inv_c_r - du) * rough_inverse(inv_c_l + inv_c_r)
    star = jnp.maximum(star, floor)

    def jump(star, p, inv_c, slope):
        r = lax.rsqrt((1.0 - RATIO) + slope * star)
        t = inv_c * r
        return (star - p) * t, r, t

    for _ in range(RIEMANN_ITERS):
        f_l, r_l, t_l = jump(star, p_l, inv_c_l, slope_l)
        f_r, r_r, t_r = jump(star, p_r, inv_c_r, slope_r)
        twice = t_l * (1.0 + r_l * r_l) + t_r * (1.0 + r_r * r_r)
        total = du + f_l + f_r
        star = star - (total + total) * rough_inverse(twice)
        star = jnp.maximum(star, floor)
    f_l, _, _ = jump(star, p_l, inv_c_l, slope_l)
    f_r, _, _ = jump(star, p_r, inv_c_r, slope_r)
    speed = 0.5 * ((u_l - f_l) + (u_r + f_r))
    up = speed > 0.0
    vel = [speed if a == normal else jnp.where(up, left[a], right[a]) for a in (2, 3, 4)]
    rho = jnp.where(up, rho_l, rho_r)
    press = jnp.where(up, p_l, p_r)
    energy = press * (1.0 / (GAMMA - 1.0)) + 0.5 * rho * (
        vel[0] * vel[0] + vel[1] * vel[1] + vel[2] * vel[2]
    )
    mass = rho * speed
    flux = [mass, (energy + star) * speed] + [mass * v for v in vel]
    flux[normal] = flux[normal] + star
    return flux


def advance(cells, low, high):
    rho, press = cells[0], cells[1]
    vel = cells[2:5]
    energy = press * (1.0 / (GAMMA - 1.0)) + 0.5 * rho * (
        vel[0] * vel[0] + vel[1] * vel[1] + vel[2] * vel[2]
    )
    old = [rho, energy] + [rho * v for v in vel]
    new = [o - COURANT * (h - l) for o, h, l in zip(old, high, low)]
    rho = jnp.maximum(new[0], DENS_FLOOR)
    inv = inverse(rho)
    vel = [m * inv for m in new[2:5]]
    press = (GAMMA - 1.0) * (
        new[1] - 0.5 * rho * (vel[0] * vel[0] + vel[1] * vel[1] + vel[2] * vel[2])
    )
    return [rho, jnp.maximum(press, PRESS_FLOOR)] + vel


def lane_roll(a, shift):
    if shift % LANES == 0:
        return a
    flat = a.reshape(-1, LANES)
    return pltpu.roll(flat, shift % LANES, 1).reshape(a.shape)


def from_below(a, fill):
    lane = lax.broadcasted_iota(jnp.int32, a.shape, 3)
    rolled = lane_roll(a, 1)
    other = jnp.concatenate([fill, rolled[:, :-1]], axis=1)
    return jnp.where(lane == 0, other, rolled)


def from_above(a, fill):
    lane = lax.broadcasted_iota(jnp.int32, a.shape, 3)
    rolled = lane_roll(a, LANES - 1)
    other = jnp.concatenate([rolled[:, 1:], fill], axis=1)
    return jnp.where(lane == LANES - 1, other, rolled)


def x_sweep(cells, sign_low, sign_high):
    rows, halves = cells[0].shape[:2]
    lane = lax.broadcasted_iota(jnp.int32, (1, SUBS, LANES), 2)
    left, right = [], []
    for f, a in enumerate(cells):
        s_low = sign_low if f == 2 else 1.0
        s_high = sign_high if f == 2 else 1.0
        below = from_below(a, s_low * a[:, :1])
        above = from_above(a, s_high * a[:, -1:])
        above2 = from_above(above, s_high * below[:, -1:])
        upper = interface(below, a, above, above2)
        lower = from_below(upper, 0.5 * (a[:, :1] + s_low * a[:, :1]))
        west, east = edge_pair(a, lower, upper)
        west_next = from_above(west, s_high * east[:, -1:])
        first = west[0, :1]
        for r in range(1, rows):
            first = jnp.where(lane == r, lane_roll(west[r, :1], r), first)
        count = rows * halves
        left.append(
            jnp.concatenate([east.reshape(count, SUBS, LANES), s_low * first], axis=0)
        )
        right.append(jnp.concatenate([west_next.reshape(count, SUBS, LANES), first], axis=0))
    flux = riemann_flux(left, right, 2)
    low, high = [], []
    for f in range(FIELDS):
        upper = flux[f][:-1].reshape(rows, halves, SUBS, LANES)
        faces = flux[f][-1:]
        fill = jnp.stack([lane_roll(faces, -r) for r in range(rows)], axis=0)
        low.append(from_below(upper, fill))
        high.append(upper)
    return advance(cells, low, high)


def line_flux(cells, normal):
    left, right = [], []
    for a in cells:
        inter = interface(a[:, :-3], a[:, 1:-2], a[:, 2:-1], a[:, 3:])
        west, east = edge_pair(a[:, 2:-2], inter[:, :-1], inter[:, 1:])
        left.append(east[:, :-1])
        right.append(west[:, 1:])
    return riemann_flux(left, right, normal)


def view(refs, cells, f, h):
    start = max(f - 2, 0) * cells
    return refs[min(f, 2)].at[pl.ds(start, cells), pl.ds(h * LANES, LANES)]


def block(get, h, start, stop):
    return [
        jnp.stack([get(h, j, f) for j in range(start, stop)], axis=0) for f in range(FIELDS)
    ]


def z_tile(zpad, h, j, f):
    return zpad[h, pl.ds((j * FIELDS + f) * SUBS, SUBS), :]


def inner_faces(get, halves, count, normal):
    blocks = [block(get, h, 3, count + 3) for h in range(halves)]
    return line_flux([jnp.stack(a, axis=0) for a in zip(*blocks)], normal)


def finished(get, h, count, normal, inner):
    ends = [block(get, h, 0, 8), block(get, h, count - 2, count + 6)]
    outer = line_flux([jnp.stack(a, axis=0) for a in zip(*ends)], normal)
    faces = [jnp.concatenate([o[0], i, o[1]], axis=0) for o, i in zip(outer, inner)]
    own = block(get, h, 3, count + 3)
    return advance(own, [a[:-1] for a in faces], [a[1:] for a in faces])


def last_kernel(sizes, zpad, inner, done, dens_out, press_out, vel_out, mine, out_sem):
    planes, rows, halves = sizes
    cells, last = planes * rows, halves - 1

    def out_copy(f, h):
        return pltpu.make_async_copy(
            mine.at[f] if h == last else done.at[f, h],
            view((dens_out, press_out, vel_out), cells, f, h),
            out_sem.at[f, h],
        )

    for h in range(last):
        for f in range(FIELDS):
            out_copy(f, h).start()
    new = finished(
        functools.partial(z_tile, zpad), last, planes, 4, [inner[f] for f in range(FIELDS)]
    )
    for f in range(FIELDS):
        mine[f] = new[f].reshape(cells, LANES)
        out_copy(f, last).start()
    for h in range(halves):
        for f in range(FIELDS):
            out_copy(f, h).wait()


def kernel(
    sizes,
    flags_in,
    dens_in,
    press_in,
    vel_in,
    zpad,
    inner_out,
    done,
    flags,
    held,
    ypad,
    flag_sem,
    in_sem,
    y_send,
    y_recv,
    z_send,
    z_recv,
):
    planes, rows, halves = sizes
    cells = planes * rows
    step = FIELDS * SUBS
    row, row_count = lax.axis_index("row"), lax.axis_size("row")
    gz, gz_count = lax.axis_index("gz"), lax.axis_size("gz")

    loads = [
        pltpu.make_async_copy(
            view((dens_in, press_in, vel_in), cells, f, h), held.at[f, h], in_sem.at[f, h]
        )
        for f in range(FIELDS)
        for h in range(halves)
    ]
    loads.append(pltpu.make_async_copy(flags_in, flags, flag_sem))
    for copy in loads:
        copy.start()

    barrier = pltpu.get_barrier_semaphore()
    sides = (
        (row > 0, {"row": row - 1}),
        (row < row_count - 1, {"row": row + 1}),
        (gz > 0, {"gz": gz - 1}),
        (gz < gz_count - 1, {"gz": gz + 1}),
    )
    for there, device in sides:

        @pl.when(there)
        def _(device=device):
            pl.semaphore_signal(
                barrier, inc=1, device_id=device, device_id_type=pl.DeviceIdType.MESH
            )

    for copy in loads:
        copy.wait()

    signs = [jnp.where(flags[k] == 1, -1.0, 1.0).astype(jnp.float32) for k in range(6)]

    def swept_rows(which):
        here = [
            jnp.stack(
                [
                    jnp.stack(
                        [held[f, h, pl.ds(r, SUBS, stride=rows), :] for h in range(halves)],
                        axis=0,
                    )
                    for r in which
                ],
                axis=0,
            )
            for f in range(FIELDS)
        ]
        new = x_sweep(here, signs[0], signs[1])
        for f in range(FIELDS):
            for i, r in enumerate(which):
                for h in range(halves):
                    ypad[h, 3 + r, f] = new[f][i, h]

    def y_copy(up, h):
        source, target = (rows, 0) if up else (3, rows + 3)
        return pltpu.make_async_remote_copy(
            src_ref=ypad.at[h, pl.ds(source, 3)],
            dst_ref=ypad.at[h, pl.ds(target, 3)],
            send_sem=y_send.at[up, h],
            recv_sem=y_recv.at[up, h],
            device_id={"row": row + (1 if up else -1)},
            device_id_type=pl.DeviceIdType.MESH,
        )

    def z_copy(up, h):
        source, target = (planes, 0) if up else (3, planes + 3)
        return pltpu.make_async_remote_copy(
            src_ref=zpad.at[h, pl.ds(source * step, 3 * step)],
            dst_ref=zpad.at[h, pl.ds(target * step, 3 * step)],
            send_sem=z_send.at[up, h],
            recv_sem=z_recv.at[up, h],
            device_id={"gz": gz + (1 if up else -1)},
            device_id_type=pl.DeviceIdType.MESH,
        )

    row_up, row_down = row < row_count - 1, row > 0
    gz_up, gz_down = gz < gz_count - 1, gz > 0

    odd = row % 2 == 1
    first = (row % 2) * (rows - 3)
    second = (rows - 3) - first

    def send_rows(up, when):
        @pl.when(when)
        def _():
            for h in range(halves):
                y_copy(up, h).start()

    swept_rows([first + i for i in range(3)])
    pl.semaphore_wait(barrier, sum(there.astype(jnp.int32) for there, _ in sides))
    send_rows(1, jnp.logical_and(row_up, odd))
    send_rows(0, jnp.logical_and(row_down, jnp.logical_not(odd)))
    swept_rows([second + i for i in range(3)])
    send_rows(1, jnp.logical_and(row_up, jnp.logical_not(odd)))
    send_rows(0, jnp.logical_and(row_down, odd))
    swept_rows(list(range(3, rows - 3)))

    def ghosts(get, put, count, normal, sign, upper):
        for f in range(FIELDS):
            for k in (1, 2, 3):
                inside = count + 3 - k if upper else 2 + k
                edge = count + 2 if upper else 3
                outside = count + 2 + k if upper else 3 - k
                mirror = get(inside, f)
                if f == normal:
                    mirror = -mirror
                put(outside, f, jnp.where(sign < 0.0, mirror, get(edge, f)))

    def y_get(h, j, f):
        return ypad[h, j, f]

    def y_put(h, j, f, value):
        ypad[h, j, f] = value

    z_get = functools.partial(z_tile, zpad)

    def z_put(h, j, f, value):
        zpad[h, pl.ds(j * step + f * SUBS, SUBS), :] = value

    def arrival(copy, get, put, down, up, count, normal, sign_low, sign_high, h):
        @pl.when(down)
        def _():
            copy(1, h).wait_recv()

        @pl.when(jnp.logical_not(down))
        def _():
            ghosts(
                functools.partial(get, h),
                functools.partial(put, h),
                count,
                normal,
                sign_low,
                False,
            )

        @pl.when(up)
        def _():
            copy(0, h).wait_recv()

        @pl.when(jnp.logical_not(up))
        def _():
            ghosts(
                functools.partial(get, h),
                functools.partial(put, h),
                count,
                normal,
                sign_high,
                True,
            )

    even_gz = gz % 2 == 0

    def send_planes(up, h, when):
        @pl.when(when)
        def _():
            z_copy(up, h).start()

    def y_finish(h, new):
        for f in range(FIELDS):
            for r in range(rows):
                zpad[h, pl.ds(3 * step + f * SUBS + r, planes, stride=step), :] = new[f][r]

        send_planes(1, h, jnp.logical_and(gz_up, even_gz))
        send_planes(0, h, gz_down)
        send_planes(1, h, jnp.logical_and(gz_up, jnp.logical_not(even_gz)))

    inner = inner_faces(y_get, halves, rows, 3)
    for h in range(halves):
        arrival(y_copy, y_get, y_put, row_down, row_up, rows, 3, signs[2], signs[3], h)
        y_finish(h, finished(y_get, h, rows, 3, [i[h] for i in inner]))

    inner = inner_faces(z_get, halves, planes, 4)
    for f in range(FIELDS):
        inner_out[f] = inner[f][halves - 1]
    for h in range(halves):
        arrival(z_copy, z_get, z_put, gz_down, gz_up, planes, 4, signs[4], signs[5], h)
        if h < halves - 1:
            new = finished(z_get, h, planes, 4, [i[h] for i in inner])
            for f in range(FIELDS):
                done[f, h] = new[f].reshape(cells, LANES)

    for there, copy, up in (
        (row_up, y_copy, 1),
        (row_down, y_copy, 0),
        (gz_up, z_copy, 1),
        (gz_down, z_copy, 0),
    ):

        @pl.when(there)
        def _(copy=copy, up=up):
            for h in range(halves):
                copy(up, h).wait_send()


def on_device(density, pressure, velocity, boundary):
    planes, rows, width = density.shape
    cells, halves = planes * rows, width // LANES
    sizes = (planes, rows, halves)
    scalar = pltpu.HBM((cells, width), jnp.float32)
    vector = pltpu.HBM((3 * cells, width), jnp.float32)
    hbm = pl.BlockSpec(memory_space=pltpu.HBM)
    vmem = pl.BlockSpec(memory_space=pltpu.VMEM)
    between = pl.pallas_call(
        functools.partial(kernel, sizes),
        out_shape=(
            pltpu.VMEM((halves, (planes + 6) * FIELDS * rows, LANES), jnp.float32),
            pltpu.VMEM((FIELDS, planes - 5, rows, LANES), jnp.float32),
            pltpu.VMEM((FIELDS, halves - 1, cells, LANES), jnp.float32),
        ),
        in_specs=[hbm] * 4,
        out_specs=(vmem, vmem, vmem),
        scratch_shapes=[
            pltpu.SMEM((6,), jnp.int32),
            pltpu.VMEM((FIELDS, halves, cells, LANES), jnp.float32),
            pltpu.VMEM((halves, rows + 6, FIELDS, planes, LANES), jnp.float32),
            pltpu.SemaphoreType.DMA(()),
            pltpu.SemaphoreType.DMA((FIELDS, halves)),
            pltpu.SemaphoreType.DMA((2, halves)),
            pltpu.SemaphoreType.DMA((2, halves)),
            pltpu.SemaphoreType.DMA((2, halves)),
            pltpu.SemaphoreType.DMA((2, halves)),
        ],
        compiler_params=pltpu.CompilerParams(
            collective_id=0, has_side_effects=True, vmem_limit_bytes=LIMIT
        ),
    )(
        boundary,
        density.reshape(cells, width),
        pressure.reshape(cells, width),
        velocity.reshape(3 * cells, width),
    )
    dens, press, vel = pl.pallas_call(
        functools.partial(last_kernel, sizes),
        out_shape=(scalar, scalar, vector),
        in_specs=[vmem] * 3,
        out_specs=(hbm, hbm, hbm),
        scratch_shapes=[
            pltpu.VMEM((FIELDS, cells, LANES), jnp.float32),
            pltpu.SemaphoreType.DMA((FIELDS, halves)),
        ],
        compiler_params=pltpu.CompilerParams(vmem_limit_bytes=16 * 1024 * 1024),
    )(*between)
    return (
        dens.reshape(planes, rows, width),
        press.reshape(planes, rows, width),
        vel.reshape(3, planes, rows, width),
    )


def solution(mesh):
    in_specs = (P("gz", "row", None), P("gz", "row", None), P(None, "gz", "row", None), P())
    out_specs = (P("gz", "row", None), P("gz", "row", None), P(None, "gz", "row", None))
    return jax.shard_map(
        on_device, mesh=mesh, in_specs=in_specs, out_specs=out_specs, check_vma=False
    )
```
